256 devices in a mesh: head: 8 (over z), seq: 32 (over x, y, core).
Axes of the slice: x: 4, y: 4, z: 8, core: 2. Of those that a mesh axis runs over, the one named last changes fastest.
Arguments:
- queries: bfloat16 [32768, 8192], P(('seq', 'head')), may hold values from -6 to 6
- key_rows: bfloat16 [32768, 8192], P(('seq', 'head')), may hold values from -0.5390625 to 0.5390625
- value_rows: bfloat16 [32768, 8192], P(('seq', 'head')), may hold values from -6 to 6
- log_decay: float32 [32768, 64], P('seq', 'head'), may hold values from -1 to 0, as said below
- initial_state: float32 [64, 128, 128], P('head'), may hold values from -24 to 24
Outputs:
- attended: bfloat16 [32768, 8192], P(('seq', 'head'))
The draws below stay inside these ranges and needn't reach their ends.
Inputs may be any that keep to these rules, and one draw needn't show every extreme that they name: `log_decay`: entries are negative.
All inputs are finite; a program needn't handle non-finite values.
Results may differ from the reference program's by a relative error of at most 0.005.
Values may be sent and summed in bfloat16 or wider, within the bound.
No kernel may reach another device: no remote copies, remote signals or barrier semaphores. Data moves between devices by JAX's collectives and lax.ppermute only.
A program may use at most 128 MiB of HBM per device.

```python
import jax
import jax.numpy as jnp
from jax import lax

H = 64
DH = 128
BLOCK = 256
TOKENS = 32768


def draw_log_decay(key, part):
    key = jax.random.fold_in(key, 7)
    keys_all = jax.random.split(key, 6)
    share = 0.5
    picked = jax.random.uniform(keys_all[0], (H,))
    fast_heads = picked < share
    fast_rate = jnp.exp(jax.random.uniform(keys_all[1], (H,), minval=jnp.log(1.0 / 50.0), maxval=jnp.log(1.0 / 30.0)))
    slow_rate = jnp.exp(jax.random.uniform(keys_all[2], (H,), minval=jnp.log(0.05), maxval=jnp.log(0.5))) / TOKENS
    forgetting_factors = jnp.where(fast_heads, fast_rate, slow_rate)
    stochastic_shift = jnp.exp(jax.random.uniform(keys_all[3], (TOKENS, H), minval=-0.7, maxval=0.7))
    marked_locations = jax.random.randint(keys_all[4], (3,), 0, TOKENS)
    fading_magnitudes = jnp.log(jax.random.uniform(keys_all[5], (3,), minval=0.5, maxval=0.8))
    location_indices = jnp.arange(TOKENS, dtype=jnp.int32)
    sudden_interval_lengths = jnp.sum(jnp.where(location_indices[:, None] == marked_locations[None, :], fading_magnitudes[None, :], 0.0), axis=1)
    return (-forgetting_factors[None, :] * stochastic_shift + sudden_interval_lengths[:, None]).astype(jnp.float32)


def level_of(key, extent, cuts, least, high):
    gain = 1.0
    for position, shards_of in cuts:
        heights = jax.random.uniform(jax.random.fold_in(jax.random.fold_in(key, 6), position), (shards_of,), jnp.float32, least / len(cuts), high / len(cuts))
        gain = gain * jnp.repeat(jnp.exp(heights), extent[position] // shards_of).reshape((-1,) + (1,) * (len(extent) - 1 - position))
    return gain


def bell_draw(rng, dims, deviation, bound, shards=(), held_as=jnp.bfloat16):
    level = level_of(rng, dims, shards, -0.22, 0.18) if shards else 1.0
    entries = jax.random.normal(rng, dims, jnp.float32) * deviation * level
    return jnp.minimum(jnp.maximum(entries, -bound), bound).astype(held_as)


def setup_inputs(seed: int = 0) -> dict:
    keys = jax.random.split(jax.random.key(seed), 6)
    return {
        "queries": bell_draw(keys[0], (TOKENS, H * DH), 1.0, 6.0, ((0, 256),)),
        "key_rows": bell_draw(keys[1], (TOKENS, H * DH), 0.09, 0.5390625, ((0, 256),)),
        "value_rows": bell_draw(keys[2], (TOKENS, H * DH), 1.0, 6.0, ((0, 256),)),
        "log_decay": draw_log_decay(jax.random.fold_in(keys[5], 71), 0),
        "initial_state": bell_draw(keys[4], (H, DH, DH), 4.0, 24.0, ((0, 8),), jnp.float32),
    }


HIGHEST = lax.Precision.HIGHEST

def reference(queries, key_rows, value_rows, log_decay, initial_state):
    block_count = TOKENS // BLOCK
    q_blocks = queries.reshape(block_count, BLOCK, H, DH)
    k_blocks = key_rows.reshape(block_count, BLOCK, H, DH)
    v_blocks = value_rows.reshape(block_count, BLOCK, H, DH)
    d_blocks = log_decay.reshape(block_count, BLOCK, H)
    rowsidx = jnp.arange(BLOCK, dtype=jnp.int32)
    causal = rowsidx[:, None] >= rowsidx[None, :]

    def advance(state, pieces):
        q_piece, k_piece, v_piece, decays = pieces
        query_f32 = q_piece.astype(jnp.float32)
        key_f32 = k_piece.astype(jnp.float32)
        value_f32 = v_piece.astype(jnp.float32)
        cum_decay = jnp.cumsum(decays, axis=0)
        per_head_values = cum_decay.T
        gaps = per_head_values[:, :, None] - per_head_values[:, None, :]
        weight = jnp.where(causal[None], jnp.exp(jnp.minimum(gaps, 0.0)), 0.0)
        scores = jnp.einsum('ihd,jhd->hij', query_f32, key_f32, precision=HIGHEST)
        result = jnp.einsum('hij,jhd->ihd', scores * weight, value_f32, precision=HIGHEST)
        result = result + jnp.exp(cum_decay)[:, :, None] * jnp.einsum('ihd,hde->ihe', query_f32, state, precision=HIGHEST)
        closing_running_total = cum_decay[-1]
        carried = jnp.exp(closing_running_total[None, :] - cum_decay)
        state = jnp.exp(closing_running_total)[:, None, None] * state + jnp.einsum('jhd,jhe->hde', key_f32 * carried[:, :, None], value_f32, precision=HIGHEST)
        factor = lax.rsqrt(lax.optimization_barrier(jnp.mean(result * result, axis=-1, keepdims=True)) + 1e-05)
        return (state, (result * factor).astype(jnp.bfloat16))
    _, outputs = lax.scan(advance, initial_state, (q_blocks, k_blocks, v_blocks, d_blocks))
    return outputs.reshape(TOKENS, H * DH)
```

```python
import functools

import jax
import jax.numpy as jnp
from jax import lax
from jax.experimental import pallas as pl
from jax.experimental.pallas import tpu as pltpu
from jax.sharding import PartitionSpec as P

DH = 128
ROWS = 128
GROUP = 8
HALVES = 2
PART = GROUP // HALVES
NZ = 8
NS = 32
WIDE = PART * DH
VMEM = 48 * 1024 * 1024
HIGHEST = lax.Precision.HIGHEST
F32 = jnp.float32
BF16 = jnp.bfloat16
ORDER = (4, 3, 5, 2, 6, 1, 7, 0)


def params():
    return pltpu.CompilerParams(vmem_limit_bytes=VMEM)


def split(x):
    hi = x.astype(BF16)
    return hi, (x - hi.astype(F32)).astype(BF16)


def dot(a, b, dims):
    return lax.dot_general(a, b, (dims, ((), ())), preferred_element_type=F32)


def iota2(axis):
    return lax.broadcasted_iota(jnp.int32, (ROWS, ROWS), axis)


def state_kernel(half, zi, k_ref, v_ref, ld_ref, out_ref):
    later = (iota2(1) > iota2(0)).astype(F32)
    suffix = lax.dot_general(
        later, ld_ref[0], (((1,), (0,)), ((), ())), precision=HIGHEST, preferred_element_type=F32
    )
    carried = jnp.exp(jnp.minimum(suffix, 0.0))
    for i in range(PART):
        cols = slice(i * DH, (i + 1) * DH)
        h = half * PART + i
        hi, lo = split(k_ref[:, cols].astype(F32) * carried[:, h : h + 1])
        v = v_ref[:, cols]
        out_ref[i] = (dot(hi, v, ((0,), (0,))) + dot(lo, v, ((0,), (0,)))).astype(out_ref.dtype)


def block_state(half, turn, zi, k, v, ld8):
    def chunk(i, zr):
        return lax.rem(zr[0] + turn, NZ)

    return pl.pallas_call(
        functools.partial(state_kernel, half),
        grid_spec=pltpu.PrefetchScalarGridSpec(
            num_scalar_prefetch=1,
            grid=(1,),
            in_specs=[
                pl.BlockSpec((ROWS, WIDE), lambda i, zr: (0, chunk(i, zr) * HALVES + half)),
                pl.BlockSpec((ROWS, WIDE), lambda i, zr: (0, chunk(i, zr) * HALVES + half)),
                pl.BlockSpec((1, ROWS, GROUP), lambda i, zr: (chunk(i, zr), 0, 0)),
            ],
            out_specs=pl.BlockSpec((PART, DH, DH), lambda i, zr: (0, 0, 0)),
        ),
        out_shape=jax.ShapeDtypeStruct((PART, DH, DH), BF16),
        compiler_params=params(),
        cost_estimate=pl.CostEstimate(flops=4 * PART * ROWS * DH * DH, bytes_accessed=400000, transcendentals=1024),
    )(zi, k, v, ld8)


def intra_kernel(q_ref, k_ref, v_ref, ld_ref, ldt_ref, out_ref, ec_ref):
    upto = (iota2(1) <= iota2(0)).astype(F32)
    cum = lax.dot_general(
        upto, ld_ref[0], (((1,), (0,)), ((), ())), precision=HIGHEST, preferred_element_type=F32
    )
    cum_t = lax.dot_general(
        ldt_ref[0], upto, (((1,), (1,)), ((), ())), precision=HIGHEST, preferred_element_type=F32
    )
    ec_ref[0] = jnp.exp(cum)
    causal = iota2(0) >= iota2(1)
    for i in range(GROUP):
        cols = slice(i * DH, (i + 1) * DH)
        gaps = cum[:, i : i + 1] - cum_t[i : i + 1, :]
        weight = jnp.where(causal, jnp.exp(jnp.minimum(gaps, 0.0)), 0.0)
        scores = dot(q_ref[:, cols], k_ref[:, cols], ((1,), (1,)))
        hi, lo = split(scores * weight)
        v = v_ref[:, cols]
        out_ref[:, cols] = dot(hi, v, ((1,), (0,))) + dot(lo, v, ((1,), (0,)))


def intra(q, k, v, ld8, ld8t):
    wide = GROUP * DH
    block = pl.BlockSpec((ROWS, wide), lambda i: (0, i))
    return pl.pallas_call(
        intra_kernel,
        grid=(NZ,),
        in_specs=[
            block,
            block,
            block,
            pl.BlockSpec((1, ROWS, GROUP), lambda i: (i, 0, 0)),
            pl.BlockSpec((1, GROUP, ROWS), lambda i: (i, 0, 0)),
        ],
        out_specs=[block, pl.BlockSpec((1, ROWS, GROUP), lambda i: (i, 0, 0))],
        out_shape=[
            jax.ShapeDtypeStruct((ROWS, NZ * wide), F32),
            jax.ShapeDtypeStruct((NZ, ROWS, GROUP), F32),
        ],
        compiler_params=params(),
        cost_estimate=pl.CostEstimate(flops=64 * 6 * 128**3, bytes_accessed=10 << 20, transcendentals=1 << 20),
    )(q, k, v, ld8, ld8t)


def spread_kernel(w_ref, *refs):
    states, entry_ref, outs = refs[:NZ], refs[NZ], refs[NZ + 1 :]

    def tile(t, _):
        rows = pl.ds(pl.multiple_of(t * 32, 32), 32)
        for h in range(PART):
            parts = [s[h, rows, :].astype(F32) for s in states] + [entry_ref[h, rows, :]]
            for k in range(NZ):
                base = (h * NZ + k) * (NZ + 1)
                total = parts[0] * w_ref[base]
                for j in range(1, NZ + 1):
                    total = total + parts[j] * w_ref[base + j]
                outs[k][h, rows, :] = total.astype(BF16)
        return 0

    lax.fori_loop(0, DH // 32, tile, 0)


def spread(weights, states, entry):
    vm = pl.BlockSpec(memory_space=pltpu.VMEM)
    return pl.pallas_call(
        spread_kernel,
        in_specs=[pl.BlockSpec(memory_space=pltpu.SMEM)] + [vm] * (NZ + 1),
        out_specs=[vm] * NZ,
        out_shape=[jax.ShapeDtypeStruct((PART, DH, DH), BF16)] * NZ,
        compiler_params=params(),
        cost_estimate=pl.CostEstimate(flops=PART * DH * DH * 144, bytes_accessed=3 << 20, transcendentals=0),
    )(weights.reshape(-1), *states, entry)


def finish_kernel(half, zi, q_ref, o_ref, ec_ref, e_ref, *rest):
    out_ref = rest[-1]
    for i in range(PART):
        cols = slice(i * DH, (i + 1) * DH)
        h = half * PART + i
        o = o_ref[:, cols] + ec_ref[0, :, h : h + 1] * dot(q_ref[:, cols], e_ref[i], ((1,), (0,)))
        factor = lax.rsqrt(jnp.mean(o * o, axis=-1, keepdims=True) + 1e-5)
        out_ref[:, cols] = (o * factor).astype(BF16)


def finish(half, turn, zi, q, o, ec, entry, held):
    def chunk(zr):
        return lax.rem(zr[0] + NZ - turn, NZ)

    wide = pl.BlockSpec((ROWS, WIDE), lambda i, zr: (0, chunk(zr) * HALVES + half))
    specs = [
        wide,
        wide,
        pl.BlockSpec((1, ROWS, GROUP), lambda i, zr: (chunk(zr), 0, 0)),
        pl.BlockSpec((PART, DH, DH), lambda i, zr: (0, 0, 0)),
    ]
    args = [zi, q, o, ec, entry]
    aliases = {}
    if held is not None:
        specs.append(pl.BlockSpec(memory_space=pl.ANY))
        args.append(held)
        aliases = {5: 0}
    return pl.pallas_call(
        functools.partial(finish_kernel, half),
        grid_spec=pltpu.PrefetchScalarGridSpec(
            num_scalar_prefetch=1,
            grid=(1,),
            in_specs=specs,
            out_specs=wide,
        ),
        out_shape=jax.ShapeDtypeStruct(q.shape, BF16),
        input_output_aliases=aliases,
        compiler_params=params(),
        cost_estimate=pl.CostEstimate(flops=PART * 2 * 128**3, bytes_accessed=800000, transcendentals=512),
    )(*args)


def turn_z(x, k):
    return x if k == 0 else lax.ppermute(x, "head", [(i, (i + k) % NZ) for i in range(NZ)])


def row_weights(total, z):
    edge = jnp.concatenate([jnp.zeros((1, GROUP), F32), jnp.cumsum(total, axis=0)])
    turn = jnp.arange(NZ)
    src = (z - turn) % NZ
    dst = (z + turn) % NZ
    after = edge[src + 1]
    before = edge[dst]
    gap = before[:, None, :] - after[None, :, :]
    pair = jnp.where((src[None, :] < dst[:, None])[..., None], jnp.exp(jnp.minimum(gap, 0.0)), 0.0)
    enter = jnp.exp(before)
    spreading = jnp.concatenate([pair, enter[:, None, :]], axis=1)
    closing = jnp.exp(jnp.minimum(edge[NZ][None] - after, 0.0))
    return jnp.moveaxis(spreading, 2, 0), closing


def seq_weights(sums):
    a = jnp.arange(NS)
    between = (a[None, None, :] > a[None, :, None]) & (a[None, None, :] < a[:, None, None])
    gap = jnp.sum(jnp.where(between, sums[None, None, :], 0.0), axis=-1)
    weight = jnp.where(a[None, :] < a[:, None], jnp.exp(gap), 0.0)
    first = jnp.exp(jnp.sum(jnp.where(a[None, :] < a[:, None], sums[None, :], 0.0), axis=-1))
    return weight, first


def local(queries, key_rows, value_rows, log_decay, initial_state):
    z = lax.axis_index("head").astype(jnp.int32)
    s = lax.axis_index("seq").astype(jnp.int32)
    zi = z.reshape(1)
    by_block = log_decay.reshape(NZ, ROWS, GROUP)
    ld8 = lax.all_to_all(by_block, "head", 0, 0, tiled=True)
    ld8t = jnp.swapaxes(ld8, 1, 2)

    come = []
    for half in range(HALVES):
        got = [None] * NZ
        for k in ORDER:
            got[k] = turn_z(block_state(half, k, zi, key_rows, value_rows, ld8), k)
        come.append(got)

    total = jnp.sum(by_block, axis=1)
    spreading, closing = row_weights(total, z)
    sums = lax.all_to_all(
        jnp.broadcast_to(jnp.sum(total, axis=0), (NS, GROUP)), "seq", 0, 0, tiled=True
    )
    o, ec = intra(queries, key_rows, value_rows, ld8, ld8t)

    piece = DH * PART // NS
    per_head = NS // PART
    leave = []
    for half in range(HALVES):
        heads = slice(half * PART, (half + 1) * PART)
        row_state = sum(
            closing[j, heads][:, None, None] * come[half][j].astype(F32) for j in range(NZ)
        )
        x = lax.all_to_all(row_state.reshape(NS, piece, DH), "seq", 0, 0, tiled=True)
        head = half * PART + s // per_head
        weight, first = seq_weights(lax.dynamic_index_in_dim(sums, head, 1, False))
        start = lax.dynamic_slice(
            initial_state, (head, (s % per_head) * piece, 0), (1, piece, DH)
        )
        y = jnp.dot(weight, x.reshape(NS, piece * DH), precision=HIGHEST)
        y = y.reshape(NS, piece, DH) + first[:, None, None] * start
        entry = lax.all_to_all(y, "seq", 0, 0, tiled=True).reshape(PART, DH, DH)
        leave.append(spread(spreading[heads], come[half], entry))

    out = None
    for half in range(HALVES):
        arrived = {k: turn_z(leave[half][k], k) for k in ORDER}
        for k in (0,) + ORDER[:-1]:
            out = finish(half, k, zi, queries, o, ec, arrived[k], out)
    return out


def solution(mesh):
    placed = (
        P(("seq", "head"), None),
        P(("seq", "head"), None),
        P(("seq", "head"), None),
        P("seq", "head"),
        P("head", None, None),
    )
    return jax.shard_map(
        local, mesh=mesh, in_specs=placed, out_specs=P(("seq", "head"), None), check_vma=False
    )
```

```python
import functools

import jax
import jax.numpy as jnp
from jax import lax
from jax.experimental import pallas as pl
from jax.experimental.pallas import tpu as pltpu
from jax.sharding import PartitionSpec as P

DH = 128
ROWS = 128
GROUP = 8
HEADS = 64
PAIR = GROUP // 2
NZ = 8
NX = 4
NY = 4
WIDE = GROUP * DH
LIMIT = 16 * 1024 * 1024
HIGHEST = lax.Precision.HIGHEST
F32 = jnp.float32
BF16 = jnp.bfloat16
ORDER = (4, 3, 5, 2, 6, 1, 7)
LISTED = (6, 1, 7, 4, 3, 5, 2)
SENDS = ((4, 3, 5), (2, 6, 1, 7, 0))
GROUPS = ((0, 4, 3), (5, 2, 6, 1, 7))
TAIL = 8
TAIL16 = 16


VM = pl.BlockSpec(memory_space=pltpu.VMEM)
SM = pl.BlockSpec(memory_space=pltpu.SMEM)
ANY = pl.BlockSpec(memory_space=pl.ANY)
BLOCK = pl.BlockSpec((ROWS, WIDE), lambda i: (0, i))
STATE = jax.ShapeDtypeStruct((GROUP, DH, DH), BF16)


def params():
    return pltpu.CompilerParams(vmem_limit_bytes=LIMIT)


def cost(flops, nbytes, trans=0):
    return pl.CostEstimate(flops=flops, bytes_accessed=nbytes, transcendentals=trans)


def split(x):
    hi = x.astype(BF16)
    return hi, (x - hi.astype(F32)).astype(BF16)


def dot(a, b, dims):
    return lax.dot_general(a, b, (dims, ((), ())), preferred_element_type=F32)


def iota2(axis):
    return lax.broadcasted_iota(jnp.int32, (ROWS, ROWS), axis)


def exact(a, b):
    return lax.dot_general(
        a, b, (((1,), (0,)), ((), ())), precision=HIGHEST, preferred_element_type=F32
    )


def state_kernel(count, chunks, k_ref, v_ref, ld_ref, *refs):
    outs, held, sems = refs[:count], refs[count], refs[count + 1]
    step = pl.program_id(0)
    later = (iota2(0) > iota2(1)).astype(F32)
    carried = jnp.exp(jnp.minimum(exact(ld_ref[0], later), 0.0))
    for i in range(GROUP):
        cols = slice(i * DH, (i + 1) * DH)
        hi, lo = split(k_ref[:, cols].astype(F32).T * carried[i : i + 1, :])
        v = v_ref[:, cols]
        both = jnp.concatenate([hi, lo], axis=1)
        held[step, i] = dot(both, jnp.concatenate([v, v], axis=0), ((1,), (0,))).astype(BF16)
    copies = [pltpu.make_async_copy(held.at[k], outs[k], sems.at[k]) for k in range(count)]
    for k in range(count):

        @pl.when(step == k)
        def _():
            copies[k].start()

    @pl.when(step == count - 1)
    def _():
        for copy in copies:
            copy.wait()


def block_states(chunks, count, k, v, ld):
    wide = pl.BlockSpec((ROWS, WIDE), lambda i, c: (0, c[i]))
    return pl.pallas_call(
        functools.partial(state_kernel, count),
        grid_spec=pltpu.PrefetchScalarGridSpec(
            num_scalar_prefetch=1,
            grid=(count,),
            in_specs=[wide, wide, pl.BlockSpec((1, GROUP, ROWS), lambda i, c: (c[i], 0, 0))],
            out_specs=[ANY] * count,
            scratch_shapes=[
                pltpu.VMEM((count, GROUP, DH, DH), BF16),
                pltpu.SemaphoreType.DMA((count,)),
            ],
        ),
        out_shape=[STATE] * count,
        compiler_params=params(),
        cost_estimate=cost(count * GROUP * 4 * 128**3, count * 800000, 1 << 10),
    )(chunks, k, v, ld)


def intra_kernel(q_ref, k_ref, v_ref, ld_ref, after_ref, out_ref, qd_ref):
    ld = ld_ref[0]
    cum_t = exact(ld, (iota2(0) <= iota2(1)).astype(F32))
    causal = iota2(0) >= iota2(1)
    for i in range(GROUP):
        cols = slice(i * DH, (i + 1) * DH)
        across = jnp.broadcast_to(cum_t[i : i + 1, :], (ROWS, ROWS))
        down = across.T
        weight = jnp.where(causal, jnp.exp(jnp.minimum(down - across, 0.0)), 0.0)
        q = q_ref[:, cols]
        scores = dot(q, k_ref[:, cols], ((1,), (1,)))
        hi, lo = split(scores * weight)
        v = v_ref[:, cols]
        both = jnp.concatenate([hi, lo], axis=1)
        out_ref[:, cols] = dot(both, jnp.concatenate([v, v], axis=0), ((1,), (0,)))
        hi, lo = split(q.astype(F32) * jnp.exp(down))
        qd_ref[:, 2 * i * DH : (2 * i + 1) * DH] = hi
        qd_ref[:, (2 * i + 1) * DH : (2 * i + 2) * DH] = lo


def intra(q, k, v, ld, after):
    return pl.pallas_call(
        intra_kernel,
        grid=(NZ,),
        in_specs=[BLOCK, BLOCK, BLOCK, pl.BlockSpec((1, GROUP, ROWS), lambda i: (i, 0, 0)), ANY],
        out_specs=[BLOCK, pl.BlockSpec((ROWS, 2 * WIDE), lambda i: (0, i))],
        out_shape=[
            jax.ShapeDtypeStruct((ROWS, NZ * WIDE), F32),
            jax.ShapeDtypeStruct((ROWS, 2 * NZ * WIDE), BF16),
        ],
        compiler_params=params(),
        cost_estimate=cost(64 * 6 * 128**3, 14 << 20, 1 << 21),
    )(q, k, v, ld, after)


def row_kernel(place, w_ref, r_ref, *refs):
    turns = (0,) + LISTED
    pieces, sides = refs[:NZ], refs[-2:]
    z, core = place[0], place[1]
    for ref, side in zip(sides, (core, 1 - core)):
        for i in range(PAIR):
            h = side * PAIR + i
            total = None
            for k, piece in zip(turns, pieces):
                block = lax.rem(z + NZ - k, NZ)
                term = piece[h].astype(F32) * w_ref[block * GROUP + h]
                total = term if total is None else total + term
            ref[i, :DH, :] = total
            ref[i, DH:, :] = jnp.full((TAIL, DH), r_ref[h], F32)


def row_states(place, weights, rows, pieces, after):
    shape = jax.ShapeDtypeStruct((PAIR, DH + TAIL, DH), F32)
    return pl.pallas_call(
        row_kernel,
        in_specs=[SM, SM, SM] + [VM] * NZ + [ANY],
        out_specs=[VM, VM],
        out_shape=[shape, shape],
        compiler_params=params(),
        cost_estimate=cost(GROUP * DH * DH * 16, 3 << 20),
    )(place, weights, rows, *pieces, after)


def put(ref, i, state, decay):
    hi = decay.astype(BF16).astype(F32)
    mid = (decay - hi).astype(BF16).astype(F32)
    low = decay - hi - mid
    row = lax.broadcasted_iota(jnp.int32, (TAIL16, DH), 0)
    tail = jnp.where(row == 0, hi, jnp.where(row == 1, mid, jnp.where(row == 2, low, 0.0)))
    ref[i, :DH, :] = state.astype(BF16)
    ref[i, DH:, :] = tail.astype(BF16)


def decay_of(ref, i):
    return jnp.sum(ref[i, DH:, :].astype(F32), axis=0, keepdims=True)


def picked(values, flags):
    total = jnp.zeros_like(values[0])
    for value, flag in zip(values, flags):
        total = total + jnp.where(flag, value, 0.0)
    return total


def behind(at, n):
    return [lax.rem(at + n - k, n) for k in range(n)]


def ordered(core, mine_ref, got_ref, i):
    first = jnp.where(core == 0, mine_ref[i], got_ref[i])
    second = jnp.where(core == 0, got_ref[i], mine_ref[i])
    return first[:DH], first[DH : DH + 1], second[:DH], second[DH : DH + 1]


def pair_kernel(place, mine_ref, got_ref, out_ref):
    for i in range(PAIR):
        first, over_first, second, over_second = ordered(place[1], mine_ref, got_ref, i)
        put(out_ref, i, jnp.exp(over_second) * first + second, over_first + over_second)


def line_kernel(place, *refs):
    pairs, out_ref = refs[:NY], refs[-1]
    ys = behind(place[3], NY)
    for i in range(PAIR):
        decays = [decay_of(p, i) for p in pairs]
        total = None
        for k in range(NY):
            gap = picked(decays, [other > ys[k] for other in ys])
            term = jnp.exp(gap) * pairs[k][i, :DH, :].astype(F32)
            total = term if total is None else total + term
        put(out_ref, i, total, sum(decays))


def entry_kernel(place, start_ref, mine_ref, got_ref, *refs):
    pairs, lines, (keep_ref, give_ref) = refs[:NY], refs[NY : NY + NX], refs[-2:]
    core, x, y = place[1], place[2], place[3]
    xs, ys = behind(x, NX), behind(y, NY)
    for i in range(PAIR):
        over_pairs = [decay_of(p, i) for p in pairs]
        over_lines = [decay_of(p, i) for p in lines]
        in_line = picked(over_pairs, [at < y for at in ys])
        gap = in_line + picked(over_lines, [at < x for at in xs])
        entry = jnp.exp(gap) * start_ref[core * PAIR + i]
        for k in range(1, NY):
            gap = picked(over_pairs, [(at > ys[k]) & (at < y) for at in ys])
            weight = jnp.where(ys[k] < y, jnp.exp(gap), 0.0)
            entry = entry + weight * pairs[k][i, :DH, :].astype(F32)
        for k in range(1, NX):
            gap = in_line + picked(over_lines, [(at > xs[k]) & (at < x) for at in xs])
            weight = jnp.where(xs[k] < x, jnp.exp(gap), 0.0)
            entry = entry + weight * lines[k][i, :DH, :].astype(F32)
        first, over_first, _, _ = ordered(core, mine_ref, got_ref, i)
        later = jnp.exp(over_first) * entry + first
        keep_ref[i] = jnp.where(core == 0, entry, later)
        give_ref[i] = jnp.where(core == 0, later, entry)


def small(kernel, out_shape, place, *args):
    single = not isinstance(out_shape, list)
    return pl.pallas_call(
        kernel,
        in_specs=[SM] + [VM] * len(args),
        out_specs=VM if single else [VM] * len(out_shape),
        out_shape=out_shape,
        compiler_params=params(),
        cost_estimate=cost(PAIR * DH * DH * 16, 1 << 20),
    )(place, *args)


def seq_scan(place, mine, give, start):
    message = jax.ShapeDtypeStruct((PAIR, DH + TAIL16, DH), BF16)
    state = jax.ShapeDtypeStruct((PAIR, DH, DH), F32)
    got = swap_core(give)
    pairs = around(small(pair_kernel, message, place, mine, got), from_y, NY)
    lines = around(small(line_kernel, message, place, *pairs), from_x, NX)
    keep, give = small(
        entry_kernel, [state, state], place, start, mine, got, *pairs, *lines
    )
    return keep, swap_core(give)


def spread_kernel(place, d_ref, keep_ref, got_ref, *refs):
    turns = (0,) + LISTED
    pieces, outs, states, entries = refs[:NZ], refs[NZ : 2 * NZ], refs[-2], refs[-1]
    z, core = place[0], place[1]
    for k, piece in zip(turns, pieces):
        states[lax.rem(z + NZ - k, NZ)] = piece[...]
    for ref, side in ((keep_ref, core), (got_ref, 1 - core)):
        for i in range(PAIR):
            h = side * PAIR + i
            state = ref[i]
            for j in range(NZ):
                entries[j, h] = state.astype(BF16)
                if j < NZ - 1:
                    state = state * d_ref[j * GROUP + h] + states[j, h].astype(F32)
    for k, out in zip(turns, outs):
        out[...] = entries[lax.rem(z + k, NZ)]


def spread(place, decays, keep, got, pieces):
    outs = pl.pallas_call(
        spread_kernel,
        in_specs=[SM, SM] + [VM] * (NZ + 2),
        out_specs=[VM] * NZ,
        out_shape=[STATE] * NZ,
        scratch_shapes=[pltpu.VMEM((NZ, GROUP, DH, DH), BF16)] * 2,
        compiler_params=params(),
        cost_estimate=cost(GROUP * DH * DH * 16, 5 << 20),
    )(place, decays, keep, got, *pieces)
    return dict(zip((0,) + LISTED, outs))


def finish_kernel(count, chunks, qd_ref, o_ref, *refs):
    entries, out_ref, held = refs[:count], refs[-2], refs[-1]
    step = pl.program_id(0)
    for k in range(count):

        @pl.when(step == k)
        def _():
            for i in range(GROUP):
                cols = slice(i * DH, (i + 1) * DH)
                entry = entries[k][i]
                far = dot(
                    qd_ref[:, 2 * i * DH : (2 * i + 2) * DH],
                    jnp.concatenate([entry, entry], axis=0),
                    ((1,), (0,)),
                )
                held[i * ROWS : (i + 1) * ROWS, :] = o_ref[:, cols] + far

    o = held[...]
    ones = jnp.ones((2 * DH, DH), BF16)
    mean = dot(jnp.concatenate(split(o * o), axis=1), ones, ((1,), (0,))) * (1.0 / DH)
    o = (o * lax.rsqrt(mean + 1e-5)).astype(BF16)
    for i in range(GROUP):
        out_ref[:, i * DH : (i + 1) * DH] = o[i * ROWS : (i + 1) * ROWS, :]


def finish(chunks, qd, o, entries, held):
    count = len(entries)
    wide = pl.BlockSpec((ROWS, WIDE), lambda i, c: (0, c[i]))
    specs = [pl.BlockSpec((ROWS, 2 * WIDE), lambda i, c: (0, c[i])), wide]
    specs += [pl.BlockSpec((GROUP, DH, DH), lambda i, c: (0, 0, 0))] * count
    args = [chunks, qd, o, *entries]
    aliases = {}
    if held is not None:
        specs.append(ANY)
        args.append(held)
        aliases = {len(args) - 1: 0}
    return pl.pallas_call(
        functools.partial(finish_kernel, count),
        grid_spec=pltpu.PrefetchScalarGridSpec(
            num_scalar_prefetch=1,
            grid=(count,),
            in_specs=specs,
            out_specs=wide,
            scratch_shapes=[pltpu.VMEM((GROUP * ROWS, DH), F32)],
        ),
        out_shape=jax.ShapeDtypeStruct(o.shape, BF16),
        input_output_aliases=aliases,
        compiler_params=params(),
        cost_estimate=cost(8 * count * 4 * 128**3, count * 1500000, 1 << 14),
    )(*args)


def send(pieces, turns):
    return {
        t: lax.ppermute(pieces[t], "head", [(i, (i + t) % NZ) for i in range(NZ)]) for t in turns
    }


def seq_index(x, y, core):
    return (x * NY + y) * 2 + core


def swap_core(a):
    return lax.ppermute(a, "seq", [(i, i ^ 1) for i in range(NX * NY * 2)])


def from_y(a, k):
    pairs = [
        (seq_index(x, y, c), seq_index(x, (y + k) % NY, c))
        for x in range(NX)
        for y in range(NY)
        for c in range(2)
    ]
    return lax.ppermute(a, "seq", pairs)


def from_x(a, k):
    pairs = [
        (seq_index(x, y, c), seq_index((x + k) % NX, y, c))
        for x in range(NX)
        for y in range(NY)
        for c in range(2)
    ]
    return lax.ppermute(a, "seq", pairs)


def around(a, move, n):
    return [a] + [move(a, k) for k in range(1, n)]


def local(queries, key_rows, value_rows, log_decay, initial_state):
    queries, key_rows, value_rows = (
        pltpu.with_memory_space_constraint(a, pltpu.HBM) for a in (queries, key_rows, value_rows)
    )
    z = lax.axis_index("head").astype(jnp.int32)
    s = lax.axis_index("seq").astype(jnp.int32)
    place = jnp.stack([z, s % 2, s // (2 * NY), (s // 2) % NY])
    by_block = jnp.swapaxes(log_decay.T.reshape(GROUP, NZ, ROWS), 0, 1)
    ld = lax.all_to_all(by_block, "head", 0, 0, tiled=True)

    total = jnp.sum(by_block, axis=2)
    cells = jnp.arange(NZ)
    after = (cells[None, :] > cells[:, None])[..., None]
    closing = jnp.exp(jnp.sum(jnp.where(after, total[None], 0.0), axis=1)).reshape(-1)
    decays = jnp.exp(total).reshape(-1)
    rows = jnp.sum(total, axis=0)

    states = {}
    for turns in SENDS:
        chunks = jnp.stack([(z + t) % NZ for t in turns])
        states |= zip(turns, block_states(chunks, len(turns), key_rows, value_rows, ld))
    come = send(states, ORDER)
    come = [states[0]] + [come[t] for t in LISTED]
    o, qd = intra(queries, key_rows, value_rows, ld, states[0])

    mine, give = row_states(place, closing, rows, come, qd)
    keep, got = seq_scan(place, mine, give, initial_state)
    leave = spread(place, decays, keep, got, come)
    back = send(leave, ORDER)
    back[0] = leave[0]

    out = None
    for turns in GROUPS:
        chunks = jnp.stack([(z + NZ - t) % NZ for t in turns])
        out = finish(chunks, qd, o, [back[t] for t in turns], out)
    return out


def solution(mesh):
    placed = (
        P(("seq", "head"), None),
        P(("seq", "head"), None),
        P(("seq", "head"), None),
        P("seq", "head"),
        P("head", None, None),
    )
    return jax.shard_map(
        local, mesh=mesh, in_specs=placed, out_specs=P(("seq", "head"), None), check_vma=False
    )
```

```python
import functools

import jax
import jax.numpy as jnp
from jax import lax
from jax.experimental import pallas as pl
from jax.experimental.pallas import tpu as pltpu
from jax.sharding import PartitionSpec as P

DH = 128
ROWS = 128
GROUP = 8
HEADS = 64
PAIR = GROUP // 2
NZ = 8
NX = 4
NY = 4
WIDE = GROUP * DH
LIMIT = 16 * 1024 * 1024
HIGHEST = lax.Precision.HIGHEST
F32 = jnp.float32
BF16 = jnp.bfloat16
ORDER = (4, 3, 5, 2, 6, 1, 7)
LISTED = (6, 1, 7, 4, 3, 5, 2)
SENDS = ((4, 3), (5, 2, 6, 1, 7, 0))
STEPS = (0, 1, 3, 2)
GROUPS = ((0, 4, 3), (5, 2, 6, 1, 7))
TAIL = 8
TAIL16 = 16


VM = pl.BlockSpec(memory_space=pltpu.VMEM)
SM = pl.BlockSpec(memory_space=pltpu.SMEM)
ANY = pl.BlockSpec(memory_space=pl.ANY)
BLOCK = pl.BlockSpec((ROWS, WIDE), lambda i: (0, i))
STATE = jax.ShapeDtypeStruct((GROUP, DH, DH), BF16)


def params():
    return pltpu.CompilerParams(vmem_limit_bytes=LIMIT)


def cost(flops, nbytes, trans=0):
    return pl.CostEstimate(flops=flops, bytes_accessed=nbytes, transcendentals=trans)


def split(x):
    hi = x.astype(BF16)
    return hi, (x - hi.astype(F32)).astype(BF16)


def dot(a, b, dims):
    return lax.dot_general(a, b, (dims, ((), ())), preferred_element_type=F32)


def iota2(axis):
    return lax.broadcasted_iota(jnp.int32, (ROWS, ROWS), axis)


def exact(a, b):
    return lax.dot_general(
        a, b, (((1,), (0,)), ((), ())), precision=HIGHEST, preferred_element_type=F32
    )


def state_kernel(count, chunks, k_ref, v_ref, ld_ref, *refs):
    outs, held, sems = refs[:count], refs[count], refs[count + 1]
    step = pl.program_id(0)
    later = (iota2(0) > iota2(1)).astype(F32)
    carried = jnp.exp(jnp.minimum(exact(ld_ref[0], later), 0.0))
    for i in range(GROUP):
        cols = slice(i * DH, (i + 1) * DH)
        hi, lo = split(k_ref[:, cols].astype(F32).T * carried[i : i + 1, :])
        v = v_ref[:, cols]
        both = jnp.concatenate([hi, lo], axis=1)
        held[step, i] = dot(both, jnp.concatenate([v, v], axis=0), ((1,), (0,))).astype(BF16)
    copies = [pltpu.make_async_copy(held.at[k], outs[k], sems.at[k]) for k in range(count)]
    for k in range(count):

        @pl.when(step == k)
        def _():
            copies[k].start()

    @pl.when(step == count - 1)
    def _():
        for copy in copies:
            copy.wait()


def block_states(chunks, count, k, v, ld):
    wide = pl.BlockSpec((ROWS, WIDE), lambda i, c: (0, c[i]))
    return pl.pallas_call(
        functools.partial(state_kernel, count),
        grid_spec=pltpu.PrefetchScalarGridSpec(
            num_scalar_prefetch=1,
            grid=(count,),
            in_specs=[wide, wide, pl.BlockSpec((1, GROUP, ROWS), lambda i, c: (c[i], 0, 0))],
            out_specs=[ANY] * count,
            scratch_shapes=[
                pltpu.VMEM((count, GROUP, DH, DH), BF16),
                pltpu.SemaphoreType.DMA((count,)),
            ],
        ),
        out_shape=[STATE] * count,
        compiler_params=params(),
        cost_estimate=cost(count * GROUP * 4 * 128**3, count * 800000, 1 << 10),
    )(chunks, k, v, ld)


def intra_kernel(q_ref, k_ref, v_ref, ld_ref, after_ref, out_ref, qd_ref):
    ld = ld_ref[0]
    cum_t = exact(ld, (iota2(0) <= iota2(1)).astype(F32))
    causal = iota2(0) >= iota2(1)
    for i in range(GROUP):
        cols = slice(i * DH, (i + 1) * DH)
        across = jnp.broadcast_to(cum_t[i : i + 1, :], (ROWS, ROWS))
        down = across.T
        weight = jnp.where(causal, jnp.exp(jnp.minimum(down - across, 0.0)), 0.0)
        q = q_ref[:, cols]
        scores = dot(q, k_ref[:, cols], ((1,), (1,)))
        hi, lo = split(scores * weight)
        v = v_ref[:, cols]
        both = jnp.concatenate([hi, lo], axis=1)
        out_ref[:, cols] = dot(both, jnp.concatenate([v, v], axis=0), ((1,), (0,)))
        hi, lo = split(q.astype(F32) * jnp.exp(down))
        qd_ref[:, 2 * i * DH : (2 * i + 1) * DH] = hi
        qd_ref[:, (2 * i + 1) * DH : (2 * i + 2) * DH] = lo


def intra(q, k, v, ld, after):
    return pl.pallas_call(
        intra_kernel,
        grid=(NZ,),
        in_specs=[BLOCK, BLOCK, BLOCK, pl.BlockSpec((1, GROUP, ROWS), lambda i: (i, 0, 0)), ANY],
        out_specs=[BLOCK, pl.BlockSpec((ROWS, 2 * WIDE), lambda i: (0, i))],
        out_shape=[
            jax.ShapeDtypeStruct((ROWS, NZ * WIDE), F32),
            jax.ShapeDtypeStruct((ROWS, 2 * NZ * WIDE), BF16),
        ],
        compiler_params=params(),
        cost_estimate=cost(64 * 6 * 128**3, 14 << 20, 1 << 21),
    )(q, k, v, ld, after)


def row_kernel(place, w_ref, r_ref, *refs):
    turns = (0,) + LISTED
    pieces, sides = refs[:NZ], refs[-2:]
    z, core = place[0], place[1]
    for ref, side in zip(sides, (core, 1 - core)):
        for i in range(PAIR):
            h = side * PAIR + i
            total = None
            for k, piece in zip(turns, pieces):
                block = lax.rem(z + NZ - k, NZ)
                term = piece[h].astype(F32) * w_ref[block * GROUP + h]
                total = term if total is None else total + term
            ref[i, :DH, :] = total
            ref[i, DH:, :] = jnp.full((TAIL, DH), r_ref[h], F32)


def row_states(place, weights, rows, pieces, after):
    shape = jax.ShapeDtypeStruct((PAIR, DH + TAIL, DH), F32)
    return pl.pallas_call(
        row_kernel,
        in_specs=[SM, SM, SM] + [VM] * NZ + [ANY],
        out_specs=[VM, VM],
        out_shape=[shape, shape],
        compiler_params=params(),
        cost_estimate=cost(GROUP * DH * DH * 16, 3 << 20),
    )(place, weights, rows, *pieces, after)


def put(ref, i, state, decay):
    hi = decay.astype(BF16).astype(F32)
    mid = (decay - hi).astype(BF16).astype(F32)
    low = decay - hi - mid
    row = lax.broadcasted_iota(jnp.int32, (TAIL16, DH), 0)
    tail = jnp.where(row == 0, hi, jnp.where(row == 1, mid, jnp.where(row == 2, low, 0.0)))
    ref[i, :DH, :] = state.astype(BF16)
    ref[i, DH:, :] = tail.astype(BF16)


def decay_of(ref, i):
    return jnp.sum(ref[i, DH:, :].astype(F32), axis=0, keepdims=True)


def picked(values, flags):
    total = jnp.zeros_like(values[0])
    for value, flag in zip(values, flags):
        total = total + jnp.where(flag, value, 0.0)
    return total


def behind(at, n):
    return [lax.rem(at + n - k, n) for k in STEPS]


def ordered(core, mine_ref, got_ref, i):
    first = jnp.where(core == 0, mine_ref[i], got_ref[i])
    second = jnp.where(core == 0, got_ref[i], mine_ref[i])
    return first[:DH], first[DH : DH + 1], second[:DH], second[DH : DH + 1]


def pair_kernel(place, mine_ref, got_ref, out_ref):
    for i in range(PAIR):
        first, over_first, second, over_second = ordered(place[1], mine_ref, got_ref, i)
        put(out_ref, i, jnp.exp(over_second) * first + second, over_first + over_second)


def line_kernel(place, *refs):
    pairs, out_ref = refs[:NY], refs[-1]
    ys = behind(place[3], NY)
    for i in range(PAIR):
        decays = [decay_of(p, i) for p in pairs]
        total = None
        for k in range(NY):
            gap = picked(decays, [other > ys[k] for other in ys])
            term = jnp.exp(gap) * pairs[k][i, :DH, :].astype(F32)
            total = term if total is None else total + term
        put(out_ref, i, total, sum(decays))


def entry_kernel(place, start_ref, mine_ref, got_ref, *refs):
    pairs, lines, (keep_ref, give_ref) = refs[:NY], refs[NY : NY + NX], refs[-2:]
    core, x, y = place[1], place[2], place[3]
    xs, ys = behind(x, NX), behind(y, NY)
    for i in range(PAIR):
        over_pairs = [decay_of(p, i) for p in pairs]
        over_lines = [decay_of(p, i) for p in lines]
        in_line = picked(over_pairs, [at < y for at in ys])
        gap = in_line + picked(over_lines, [at < x for at in xs])
        entry = jnp.exp(gap) * start_ref[core * PAIR + i]
        for k in range(1, NY):
            gap = picked(over_pairs, [(at > ys[k]) & (at < y) for at in ys])
            weight = jnp.where(ys[k] < y, jnp.exp(gap), 0.0)
            entry = entry + weight * pairs[k][i, :DH, :].astype(F32)
        for k in range(1, NX):
            gap = in_line + picked(over_lines, [(at > xs[k]) & (at < x) for at in xs])
            weight = jnp.where(xs[k] < x, jnp.exp(gap), 0.0)
            entry = entry + weight * lines[k][i, :DH, :].astype(F32)
        first, over_first, _, _ = ordered(core, mine_ref, got_ref, i)
        later = jnp.exp(over_first) * entry + first
        keep_ref[i] = jnp.where(core == 0, entry, later)
        give_ref[i] = jnp.where(core == 0, later, entry)


def small(kernel, out_shape, place, *args):
    single = not isinstance(out_shape, list)
    return pl.pallas_call(
        kernel,
        in_specs=[SM] + [VM] * len(args),
        out_specs=VM if single else [VM] * len(out_shape),
        out_shape=out_shape,
        compiler_params=params(),
        cost_estimate=cost(PAIR * DH * DH * 16, 1 << 20),
    )(place, *args)


def seq_scan(place, mine, give, start):
    message = jax.ShapeDtypeStruct((PAIR, DH + TAIL16, DH), BF16)
    state = jax.ShapeDtypeStruct((PAIR, DH, DH), F32)
    got = swap_core(give)
    pairs = around(small(pair_kernel, message, place, mine, got), from_y, NY)
    lines = around(small(line_kernel, message, place, *pairs), from_x, NX)
    keep, give = small(
        entry_kernel, [state, state], place, start, mine, got, *pairs, *lines
    )
    return keep, swap_core(give)


def spread_kernel(place, d_ref, keep_ref, got_ref, *refs):
    turns = (0,) + LISTED
    pieces, outs, states, entries = refs[:NZ], refs[NZ : 2 * NZ], refs[-2], refs[-1]
    z, core = place[0], place[1]
    for k, piece in zip(turns, pieces):
        states[lax.rem(z + NZ - k, NZ)] = piece[...]
    for ref, side in ((keep_ref, core), (got_ref, 1 - core)):
        for i in range(PAIR):
            h = side * PAIR + i
            state = ref[i]
            for j in range(NZ):
                entries[j, h] = state.astype(BF16)
                if j < NZ - 1:
                    state = state * d_ref[j * GROUP + h] + states[j, h].astype(F32)
    for k, out in zip(turns, outs):
        out[...] = entries[lax.rem(z + k, NZ)]


def spread(place, decays, keep, got, pieces):
    outs = pl.pallas_call(
        spread_kernel,
        in_specs=[SM, SM] + [VM] * (NZ + 2),
        out_specs=[VM] * NZ,
        out_shape=[STATE] * NZ,
        scratch_shapes=[pltpu.VMEM((NZ, GROUP, DH, DH), BF16)] * 2,
        compiler_params=params(),
        cost_estimate=cost(GROUP * DH * DH * 16, 5 << 20),
    )(place, decays, keep, got, *pieces)
    return dict(zip((0,) + LISTED, outs))


def finish_kernel(count, chunks, qd_ref, o_ref, *refs):
    entries, out_ref, held = refs[:count], refs[-2], refs[-1]
    step = pl.program_id(0)
    for k in range(count):

        @pl.when(step == k)
        def _():
            for i in range(GROUP):
                cols = slice(i * DH, (i + 1) * DH)
                entry = entries[k][i]
                far = dot(
                    qd_ref[:, 2 * i * DH : (2 * i + 2) * DH],
                    jnp.concatenate([entry, entry], axis=0),
                    ((1,), (0,)),
                )
                held[i * ROWS : (i + 1) * ROWS, :] = o_ref[:, cols] + far

    o = held[...]
    ones = jnp.ones((2 * DH, DH), BF16)
    mean = dot(jnp.concatenate(split(o * o), axis=1), ones, ((1,), (0,))) * (1.0 / DH)
    o = (o * lax.rsqrt(mean + 1e-5)).astype(BF16)
    for i in range(GROUP):
        out_ref[:, i * DH : (i + 1) * DH] = o[i * ROWS : (i + 1) * ROWS, :]


def finish(chunks, qd, o, entries, held):
    count = len(entries)
    wide = pl.BlockSpec((ROWS, WIDE), lambda i, c: (0, c[i]))
    specs = [pl.BlockSpec((ROWS, 2 * WIDE), lambda i, c: (0, c[i])), wide]
    specs += [pl.BlockSpec((GROUP, DH, DH), lambda i, c: (0, 0, 0))] * count
    args = [chunks, qd, o, *entries]
    aliases = {}
    if held is not None:
        specs.append(ANY)
        args.append(held)
        aliases = {len(args) - 1: 0}
    return pl.pallas_call(
        functools.partial(finish_kernel, count),
        grid_spec=pltpu.PrefetchScalarGridSpec(
            num_scalar_prefetch=1,
            grid=(count,),
            in_specs=specs,
            out_specs=wide,
            scratch_shapes=[pltpu.VMEM((GROUP * ROWS, DH), F32)],
        ),
        out_shape=jax.ShapeDtypeStruct(o.shape, BF16),
        input_output_aliases=aliases,
        compiler_params=params(),
        cost_estimate=cost(8 * count * 4 * 128**3, count * 1500000, 1 << 14),
    )(*args)


def send(pieces, turns):
    return {
        t: lax.ppermute(pieces[t], "head", [(i, (i + t) % NZ) for i in range(NZ)]) for t in turns
    }


def seq_index(x, y, core):
    return (x * NY + y) * 2 + core


def swap_core(a):
    return lax.ppermute(a, "seq", [(i, i ^ 1) for i in range(NX * NY * 2)])


def from_y(a, k):
    pairs = [
        (seq_index(x, y, c), seq_index(x, (y + k) % NY, c))
        for x in range(NX)
        for y in range(NY)
        for c in range(2)
    ]
    return lax.ppermute(a, "seq", pairs)


def from_x(a, k):
    pairs = [
        (seq_index(x, y, c), seq_index((x + k) % NX, y, c))
        for x in range(NX)
        for y in range(NY)
        for c in range(2)
    ]
    return lax.ppermute(a, "seq", pairs)


def around(a, move, n):
    return [a] + [move(a, k) for k in STEPS[1:]]


def local(queries, key_rows, value_rows, log_decay, initial_state):
    queries, key_rows, value_rows = (
        pltpu.with_memory_space_constraint(a, pltpu.HBM) for a in (queries, key_rows, value_rows)
    )
    z = lax.axis_index("head").astype(jnp.int32)
    s = lax.axis_index("seq").astype(jnp.int32)
    place = jnp.stack([z, s % 2, s // (2 * NY), (s // 2) % NY])
    by_block = jnp.swapaxes(log_decay.T.reshape(GROUP, NZ, ROWS), 0, 1)
    ld = lax.all_to_all(by_block, "head", 0, 0, tiled=True)

    total = jnp.sum(by_block, axis=2)
    cells = jnp.arange(NZ)
    after = (cells[None, :] > cells[:, None])[..., None]
    closing = jnp.exp(jnp.sum(jnp.where(after, total[None], 0.0), axis=1)).reshape(-1)
    decays = jnp.exp(total).reshape(-1)
    rows = jnp.sum(total, axis=0)

    states = {}
    for turns in SENDS:
        chunks = jnp.stack([(z + t) % NZ for t in turns])
        states |= zip(turns, block_states(chunks, len(turns), key_rows, value_rows, ld))
    come = send(states, ORDER)
    come = [states[0]] + [come[t] for t in LISTED]
    o, qd = intra(queries, key_rows, value_rows, ld, states[0])

    mine, give = row_states(place, closing, rows, come, qd)
    keep, got = seq_scan(place, mine, give, initial_state)
    leave = spread(place, decays, keep, got, come)
    back = send(leave, ORDER)
    back[0] = leave[0]

    out = None
    for turns in GROUPS:
        chunks = jnp.stack([(z + NZ - t) % NZ for t in turns])
        out = finish(chunks, qd, o, [back[t] for t in turns], out)
    return out


def solution(mesh):
    placed = (
        P(("seq", "head"), None),
        P(("seq", "head"), None),
        P(("seq", "head"), None),
        P("seq", "head"),
        P("head", None, None),
    )
    return jax.shard_map(
        local, mesh=mesh, in_specs=placed, out_specs=P(("seq", "head"), None), check_vma=False
    )
```

```python
import functools

import jax
import jax.numpy as jnp
from jax import lax
from jax.experimental import pallas as pl
from jax.experimental.pallas import tpu as pltpu
from jax.sharding import PartitionSpec as P

DH = 128
ROWS = 128
GROUP = 8
HEADS = 64
PAIR = GROUP // 2
NZ = 8
NX = 4
NY = 4
WIDE = GROUP * DH
LIMIT = 16 * 1024 * 1024
HIGHEST = lax.Precision.HIGHEST
F32 = jnp.float32
BF16 = jnp.bfloat16
STEPS = (0, 1, 3, 2)
FAR = (3, 2, 1)
TAIL = 8
TAIL16 = 16

VM = pl.BlockSpec(memory_space=pltpu.VMEM)
SM = pl.BlockSpec(memory_space=pltpu.SMEM)
ANY = pl.BlockSpec(memory_space=pl.ANY)
BLOCK = pl.BlockSpec((ROWS, WIDE), lambda i: (0, i))
STATE = jax.ShapeDtypeStruct((GROUP, DH, DH), BF16)


def params():
    return pltpu.CompilerParams(vmem_limit_bytes=LIMIT)


def cost(flops, nbytes, trans=0):
    return pl.CostEstimate(flops=flops, bytes_accessed=nbytes, transcendentals=trans)


def split(x):
    hi = x.astype(BF16)
    return hi, (x - hi.astype(F32)).astype(BF16)


def dot(a, b, dims):
    return lax.dot_general(a, b, (dims, ((), ())), preferred_element_type=F32)


def iota2(axis):
    return lax.broadcasted_iota(jnp.int32, (ROWS, ROWS), axis)


def exact(a, b):
    return lax.dot_general(
        a, b, (((1,), (0,)), ((), ())), precision=HIGHEST, preferred_element_type=F32
    )


def near_kernel(ld_ref, out_ref):
    for j in range(NZ):
        out_ref[j, :GROUP, :] = ld_ref[j]
        out_ref[j, GROUP:, :] = ld_ref[j ^ 1]


def with_near(ld):
    return pl.pallas_call(
        near_kernel,
        in_specs=[VM],
        out_specs=VM,
        out_shape=jax.ShapeDtypeStruct((NZ, 2 * GROUP, ROWS), F32),
        compiler_params=params(),
        cost_estimate=cost(0, 1 << 17),
    )(ld)


def state_kernel(count, chunks, k_ref, v_ref, ld_ref, *refs):
    outs, held, sems = refs[:count], refs[count], refs[count + 1]
    step = pl.program_id(0)
    later = (iota2(0) > iota2(1)).astype(F32)
    carried = jnp.exp(jnp.minimum(exact(ld_ref[0], later), 0.0))
    for i in range(GROUP):
        cols = slice(i * DH, (i + 1) * DH)
        hi, lo = split(k_ref[:, cols].astype(F32).T * carried[i : i + 1, :])
        v = v_ref[:, cols]
        both = jnp.concatenate([hi, lo], axis=1)
        held[step, i] = dot(both, jnp.concatenate([v, v], axis=0), ((1,), (0,))).astype(BF16)
    copies = [pltpu.make_async_copy(held.at[k], outs[k], sems.at[k]) for k in range(count)]
    for k in range(count):

        @pl.when(step == k)
        def _():
            copies[k].start()

    @pl.when(step == count - 1)
    def _():
        for copy in copies:
            copy.wait()


def block_states(chunks, count, k, v, ld):
    wide = pl.BlockSpec((ROWS, WIDE), lambda i, c: (0, c[i]))
    return pl.pallas_call(
        functools.partial(state_kernel, count),
        grid_spec=pltpu.PrefetchScalarGridSpec(
            num_scalar_prefetch=1,
            grid=(count,),
            in_specs=[wide, wide, pl.BlockSpec((1, GROUP, ROWS), lambda i, c: (c[i], 0, 0))],
            out_specs=[ANY] * count,
            scratch_shapes=[
                pltpu.VMEM((count, GROUP, DH, DH), BF16),
                pltpu.SemaphoreType.DMA((count,)),
            ],
        ),
        out_shape=[STATE] * count,
        compiler_params=params(),
        cost_estimate=cost(count * GROUP * 4 * 128**3, count * 800000, 1 << 10),
    )(chunks, k, v, ld)


def intra_kernel(q_ref, k_ref, v_ref, ld_ref, after_ref, out_ref, qd_ref):
    ld = ld_ref[0]
    cum_t = exact(ld, (iota2(0) <= iota2(1)).astype(F32))
    causal = iota2(0) >= iota2(1)
    for i in range(GROUP):
        cols = slice(i * DH, (i + 1) * DH)
        across = jnp.broadcast_to(cum_t[i : i + 1, :], (ROWS, ROWS))
        down = across.T
        weight = jnp.where(causal, jnp.exp(jnp.minimum(down - across, 0.0)), 0.0)
        q = q_ref[:, cols]
        scores = dot(q, k_ref[:, cols], ((1,), (1,)))
        hi, lo = split(scores * weight)
        v = v_ref[:, cols]
        both = jnp.concatenate([hi, lo], axis=1)
        out_ref[:, cols] = dot(both, jnp.concatenate([v, v], axis=0), ((1,), (0,)))
        hi, lo = split(q.astype(F32) * jnp.exp(down))
        qd_ref[:, 2 * i * DH : (2 * i + 1) * DH] = hi
        qd_ref[:, (2 * i + 1) * DH : (2 * i + 2) * DH] = lo


def intra(q, k, v, ld, after):
    return pl.pallas_call(
        intra_kernel,
        grid=(NZ,),
        in_specs=[BLOCK, BLOCK, BLOCK, pl.BlockSpec((1, GROUP, ROWS), lambda i: (i, 0, 0)), ANY],
        out_specs=[BLOCK, pl.BlockSpec((ROWS, 2 * WIDE), lambda i: (0, i))],
        out_shape=[
            jax.ShapeDtypeStruct((ROWS, NZ * WIDE), F32),
            jax.ShapeDtypeStruct((ROWS, 2 * NZ * WIDE), BF16),
        ],
        compiler_params=params(),
        cost_estimate=cost(64 * 6 * 128**3, 14 << 20, 1 << 21),
    )(q, k, v, ld, after)


def signed(place):
    return 1 - 2 * lax.rem(place[0], 2)


def group_at(place, a):
    return lax.rem(place[0] + 2 * NZ - signed(place) * a, NZ)


def pair_behind(place, a):
    own = place[0] // 2
    return lax.rem(own + 4 + {1: -1, 2: 1, 3: 2}[a] * signed(place), 4)


def join_kernel(a, place, d_ref, keep_ref, got_ref, out_ref):
    even = lax.rem(place[0], 2) == 0
    group = group_at(place, a)
    for h in range(GROUP):
        keep, got = keep_ref[h].astype(F32), got_ref[h].astype(F32)
        first, second = jnp.where(even, keep, got), jnp.where(even, got, keep)
        out_ref[h] = (first * d_ref[group * GROUP + h] + second).astype(BF16)


def join(a, place, over_odd, keep, got):
    return pl.pallas_call(
        functools.partial(join_kernel, a),
        in_specs=[SM, SM, VM, VM],
        out_specs=VM,
        out_shape=STATE,
        compiler_params=params(),
        cost_estimate=cost(GROUP * DH * DH * 4, 800000),
    )(place, over_odd, keep, got)


def part_kernel(a, place, d_ref, start_ref, keep_ref, got_ref, *refs):
    own_ref, pass_ref = refs[-2:]
    even = lax.rem(place[0], 2) == 0
    group = group_at(place, a)
    for h in range(GROUP):
        start = start_ref[h].astype(F32)
        state = jnp.where(even, keep_ref[h].astype(F32), got_ref[h].astype(F32))
        later = start * d_ref[group * GROUP + h] + state
        own_ref[h] = jnp.where(even, start, later).astype(BF16)
        pass_ref[h] = jnp.where(even, later, start).astype(BF16)


def part(a, place, over_even, start, keep, got, after):
    return pl.pallas_call(
        functools.partial(part_kernel, a),
        in_specs=[SM, SM, VM, VM, VM] + [ANY] * len(after),
        out_specs=[VM, VM],
        out_shape=[STATE, STATE],
        compiler_params=params(),
        cost_estimate=cost(GROUP * DH * DH * 4, 1300000),
    )(place, over_even, start, keep, got, *after)


def row_kernel(place, w_ref, r_ref, own_ref, near_ref, *refs):
    far, sides = refs[: len(FAR)], refs[-2:]
    z, core = place[0], place[1]
    pieces = [(own_ref, z), (near_ref, z + signed(place))]
    pieces += [(ref, 2 * pair_behind(place, a) + 1) for a, ref in zip(FAR, far)]
    for ref, side in zip(sides, (core, 1 - core)):
        for i in range(PAIR):
            h = side * PAIR + i
            total = None
            for piece, block in pieces:
                term = piece[h].astype(F32) * w_ref[block * GROUP + h]
                total = term if total is None else total + term
            ref[i, :DH, :] = total
            ref[i, DH:, :] = jnp.full((TAIL, DH), r_ref[h], F32)


def row_states(place, weights, rows, pieces):
    shape = jax.ShapeDtypeStruct((PAIR, DH + TAIL, DH), F32)
    return pl.pallas_call(
        row_kernel,
        in_specs=[SM, SM, SM] + [VM] * len(pieces),
        out_specs=[VM, VM],
        out_shape=[shape, shape],
        compiler_params=params(),
        cost_estimate=cost(GROUP * DH * DH * 10, 2 << 20),
    )(place, weights, rows, *pieces)


def put(ref, i, state, decay):
    hi = decay.astype(BF16).astype(F32)
    mid = (decay - hi).astype(BF16).astype(F32)
    low = decay - hi - mid
    row = lax.broadcasted_iota(jnp.int32, (TAIL16, DH), 0)
    tail = jnp.where(row == 0, hi, jnp.where(row == 1, mid, jnp.where(row == 2, low, 0.0)))
    ref[i, :DH, :] = state.astype(BF16)
    ref[i, DH:, :] = tail.astype(BF16)


def decay_of(ref, i):
    return jnp.sum(ref[i, DH:, :].astype(F32), axis=0, keepdims=True)


def picked(values, flags):
    total = jnp.zeros_like(values[0])
    for value, flag in zip(values, flags):
        total = total + jnp.where(flag, value, 0.0)
    return total


def behind(at, n):
    return [lax.rem(at + n - k, n) for k in STEPS]


def ordered(core, mine_ref, got_ref, i):
    first = jnp.where(core == 0, mine_ref[i], got_ref[i])
    second = jnp.where(core == 0, got_ref[i], mine_ref[i])
    return first[:DH], first[DH : DH + 1], second[:DH], second[DH : DH + 1]


def pair_kernel(place, mine_ref, got_ref, out_ref):
    for i in range(PAIR):
        first, over_first, second, over_second = ordered(place[1], mine_ref, got_ref, i)
        put(out_ref, i, jnp.exp(over_second) * first + second, over_first + over_second)


def line_kernel(place, *refs):
    pairs, out_ref = refs[:NY], refs[-1]
    ys = behind(place[3], NY)
    for i in range(PAIR):
        decays = [decay_of(p, i) for p in pairs]
        total = None
        for k in range(NY):
            gap = picked(decays, [other > ys[k] for other in ys])
            term = jnp.exp(gap) * pairs[k][i, :DH, :].astype(F32)
            total = term if total is None else total + term
        put(out_ref, i, total, sum(decays))


def entry_kernel(place, start_ref, mine_ref, got_ref, *refs):
    pairs, lines, (keep_ref, give_ref) = refs[:NY], refs[NY : NY + NX], refs[-2:]
    core, x, y = place[1], place[2], place[3]
    xs, ys = behind(x, NX), behind(y, NY)
    for i in range(PAIR):
        over_pairs = [decay_of(p, i) for p in pairs]
        over_lines = [decay_of(p, i) for p in lines]
        in_line = picked(over_pairs, [at < y for at in ys])
        gap = in_line + picked(over_lines, [at < x for at in xs])
        entry = jnp.exp(gap) * start_ref[core * PAIR + i]
        for k in range(1, NY):
            gap = picked(over_pairs, [(at > ys[k]) & (at < y) for at in ys])
            weight = jnp.where(ys[k] < y, jnp.exp(gap), 0.0)
            entry = entry + weight * pairs[k][i, :DH, :].astype(F32)
        for k in range(1, NX):
            gap = in_line + picked(over_lines, [(at > xs[k]) & (at < x) for at in xs])
            weight = jnp.where(xs[k] < x, jnp.exp(gap), 0.0)
            entry = entry + weight * lines[k][i, :DH, :].astype(F32)
        first, over_first, _, _ = ordered(core, mine_ref, got_ref, i)
        later = jnp.exp(over_first) * entry + first
        keep_ref[i] = jnp.where(core == 0, entry, later)
        give_ref[i] = jnp.where(core == 0, later, entry)


def small(kernel, out_shape, place, *args):
    single = not isinstance(out_shape, list)
    return pl.pallas_call(
        kernel,
        in_specs=[SM] + [VM] * len(args),
        out_specs=VM if single else [VM] * len(out_shape),
        out_shape=out_shape,
        compiler_params=params(),
        cost_estimate=cost(PAIR * DH * DH * 16, 1 << 20),
    )(place, *args)


def seq_scan(place, mine, give, start):
    message = jax.ShapeDtypeStruct((PAIR, DH + TAIL16, DH), BF16)
    state = jax.ShapeDtypeStruct((PAIR, DH, DH), F32)
    got = swap_core(give)
    pairs = around(small(pair_kernel, message, place, mine, got), from_y, NY)
    lines = around(small(line_kernel, message, place, *pairs), from_x, NX)
    keep, give = small(
        entry_kernel, [state, state], place, start, mine, got, *pairs, *lines
    )
    return keep, swap_core(give)


def spread_kernel(place, d_ref, keep_ref, got_ref, own_ref, near_ref, *refs):
    far, (out_own, out_near, *out_far) = refs[: len(FAR)], refs[len(FAR) : -2]
    states, entries = refs[-2], refs[-1]
    z, core = place[0], place[1]
    even, own = lax.rem(z, 2) == 0, z // 2
    for a, ref in zip(FAR, far):
        states[pair_behind(place, a)] = ref[...].astype(F32)
    for h in range(GROUP):
        mine, near = own_ref[h].astype(F32), near_ref[h].astype(F32)
        first, second = jnp.where(even, mine, near), jnp.where(even, near, mine)
        states[own, h] = first * d_ref[(2 * own + 1) * GROUP + h] + second
    for ref, side in ((keep_ref, core), (got_ref, 1 - core)):
        for i in range(PAIR):
            h = side * PAIR + i
            state = ref[i]
            for p in range(NZ // 2):
                entries[p, h] = state
                if p < NZ // 2 - 1:
                    over = d_ref[2 * p * GROUP + h] * d_ref[(2 * p + 1) * GROUP + h]
                    state = state * over + states[p, h]
    for a, out in zip(FAR, out_far):
        out[...] = entries[pair_behind(place, a)].astype(BF16)
    for h in range(GROUP):
        start = entries[own, h]
        first = jnp.where(even, own_ref[h].astype(F32), near_ref[h].astype(F32))
        later = start * d_ref[2 * own * GROUP + h] + first
        out_own[h] = jnp.where(even, start, later).astype(BF16)
        out_near[h] = jnp.where(even, later, start).astype(BF16)


def spread(place, decays, keep, got, pieces):
    count = len(pieces)
    return pl.pallas_call(
        spread_kernel,
        in_specs=[SM, SM] + [VM] * (2 + count),
        out_specs=[VM] * count,
        out_shape=[STATE] * count,
        scratch_shapes=[pltpu.VMEM((NZ // 2, GROUP, DH, DH), F32)] * 2,
        compiler_params=params(),
        cost_estimate=cost(GROUP * DH * DH * 16, 5 << 20),
    )(place, decays, keep, got, *pieces)


def finish_kernel(count, chunks, qd_ref, o_ref, *refs):
    entries, out_ref, held = refs[:count], refs[-2], refs[-1]
    step = pl.program_id(0)
    for k in range(count):

        @pl.when(step == k)
        def _():
            for i in range(GROUP):
                cols = slice(i * DH, (i + 1) * DH)
                entry = entries[k][i]
                far = dot(
                    qd_ref[:, 2 * i * DH : (2 * i + 2) * DH],
                    jnp.concatenate([entry, entry], axis=0),
                    ((1,), (0,)),
                )
                held[i * ROWS : (i + 1) * ROWS, :] = o_ref[:, cols] + far

    o = held[...]
    ones = jnp.ones((2 * DH, DH), BF16)
    mean = dot(jnp.concatenate(split(o * o), axis=1), ones, ((1,), (0,))) * (1.0 / DH)
    o = (o * lax.rsqrt(mean + 1e-5)).astype(BF16)
    for i in range(GROUP):
        out_ref[:, i * DH : (i + 1) * DH] = o[i * ROWS : (i + 1) * ROWS, :]


def finish(chunks, qd, o, entries, held):
    count = len(entries)
    wide = pl.BlockSpec((ROWS, WIDE), lambda i, c: (0, c[i]))
    specs = [pl.BlockSpec((ROWS, 2 * WIDE), lambda i, c: (0, c[i])), wide]
    specs += [pl.BlockSpec((GROUP, DH, DH), lambda i, c: (0, 0, 0))] * count
    args = [chunks, qd, o, *entries]
    aliases = {}
    if held is not None:
        specs.append(ANY)
        args.append(held)
        aliases = {len(args) - 1: 0}
    return pl.pallas_call(
        functools.partial(finish_kernel, count),
        grid_spec=pltpu.PrefetchScalarGridSpec(
            num_scalar_prefetch=1,
            grid=(count,),
            in_specs=specs,
            out_specs=wide,
            scratch_shapes=[pltpu.VMEM((GROUP * ROWS, DH), F32)],
        ),
        out_shape=jax.ShapeDtypeStruct(o.shape, BF16),
        input_output_aliases=aliases,
        compiler_params=params(),
        cost_estimate=cost(8 * count * 4 * 128**3, count * 1500000, 1 << 14),
    )(*args)


def swap_near(a):
    return lax.ppermute(a, "head", [(i, i ^ 1) for i in range(NZ)])


def hops(a):
    return [(i, (i + (a if i % 2 else -a)) % NZ) for i in range(NZ)]


def to_owner(x, a):
    return lax.ppermute(x, "head", hops(a))


def from_owner(x, a):
    return lax.ppermute(x, "head", [(j, i) for i, j in hops(a)])


def seq_index(x, y, core):
    return (x * NY + y) * 2 + core


def swap_core(a):
    return lax.ppermute(a, "seq", [(i, i ^ 1) for i in range(NX * NY * 2)])


def from_y(a, k):
    pairs = [
        (seq_index(x, y, c), seq_index(x, (y + k) % NY, c))
        for x in range(NX)
        for y in range(NY)
        for c in range(2)
    ]
    return lax.ppermute(a, "seq", pairs)


def from_x(a, k):
    pairs = [
        (seq_index(x, y, c), seq_index((x + k) % NX, y, c))
        for x in range(NX)
        for y in range(NY)
        for c in range(2)
    ]
    return lax.ppermute(a, "seq", pairs)


def around(a, move, n):
    return [a] + [move(a, k) for k in STEPS[1:]]


def local(queries, key_rows, value_rows, log_decay, initial_state):
    queries, key_rows, value_rows = (
        pltpu.with_memory_space_constraint(a, pltpu.HBM) for a in (queries, key_rows, value_rows)
    )
    z = lax.axis_index("head").astype(jnp.int32)
    s = lax.axis_index("seq").astype(jnp.int32)
    place = jnp.stack([z, s % 2, s // (2 * NY), (s // 2) % NY])
    by_block = jnp.swapaxes(log_decay.T.reshape(GROUP, NZ, ROWS), 0, 1)
    ld = lax.all_to_all(with_near(by_block), "head", 0, 0, tiled=True)

    total = jnp.sum(by_block, axis=2)
    cells = jnp.arange(NZ)
    after = (cells[None, :] > cells[:, None])[..., None]
    closing = jnp.exp(jnp.sum(jnp.where(after, total[None], 0.0), axis=1)).reshape(-1)
    decays = jnp.exp(total).reshape(-1)
    rows = jnp.sum(total, axis=0)

    sign = 1 - 2 * (z % 2)

    def keeps(*turns):
        return [(z - sign * a) % NZ for a in turns]

    def gives(*turns):
        return [(z + sign * a) % NZ for a in turns]

    over = jnp.sum(ld, axis=2)
    mine_over, near_over = over[:, :GROUP].reshape(-1), over[:, GROUP:].reshape(-1)
    over_even = jnp.exp(jnp.where(z % 2 == 0, mine_over, near_over))
    over_odd = jnp.exp(jnp.where(z % 2 == 0, near_over, mine_over))

    give, kept, got, joined = {}, {}, {}, {}
    give[4], give[3] = block_states(jnp.stack(gives(4, 3)), 2, key_rows, value_rows, ld)
    kept[3], give[2], give[1] = block_states(
        jnp.stack(keeps(3) + gives(2, 1)), 3, key_rows, value_rows, ld
    )
    kept[2], kept[1], kept[0] = block_states(
        jnp.stack(keeps(2, 1, 0)), 3, key_rows, value_rows, ld
    )
    for a in (3, 2, 1, 0):
        got[a] = swap_near(give[a + 1])
    for a in FAR:
        joined[a] = to_owner(join(a, place, over_odd, kept[a], got[a]), a)

    pieces = [kept[0], got[0]] + [joined[a] for a in FAR]
    mine, other = row_states(place, closing, rows, pieces)
    keep, other = seq_scan(place, mine, other, initial_state)
    entry = {}
    own, near, *far = spread(place, decays, keep, other, pieces)
    o, qd = intra(queries, key_rows, value_rows, ld, own)
    entry[0] = own
    near = swap_near(near)
    passed = {}
    for a, x in zip(FAR, far):
        entry[a], x = part(a, place, over_even, from_owner(x, a), kept[a], got[a], [qd])
        passed[a] = swap_near(x)

    early = [entry[0], near, entry[1], entry[2]]
    out = finish(jnp.stack(keeps(0) + gives(1) + keeps(1, 2)), qd, o, early, None)
    middle = [entry[3], passed[2], passed[1]]
    out = finish(jnp.stack(keeps(3) + gives(3, 2)), qd, o, middle, out)
    return finish(jnp.stack(gives(4)), qd, o, [passed[3]], out)


def solution(mesh):
    placed = (
        P(("seq", "head"), None),
        P(("seq", "head"), None),
        P(("seq", "head"), None),
        P("seq", "head"),
        P("head", None, None),
    )
    return jax.shard_map(
        local, mesh=mesh, in_specs=placed, out_specs=P(("seq", "head"), None), check_vma=False
    )
```

```python
import functools

import jax
import jax.numpy as jnp
from jax import lax
from jax.experimental import pallas as pl
from jax.experimental.pallas import tpu as pltpu
from jax.sharding import PartitionSpec as P

DH = 128
ROWS = 128
GROUP = 8
HEADS = 64
PAIR = GROUP // 2
NZ = 8
NX = 4
NY = 4
WIDE = GROUP * DH
LIMIT = 16 * 1024 * 1024
HIGHEST = lax.Precision.HIGHEST
F32 = jnp.float32
BF16 = jnp.bfloat16
STEPS = (0, 1, 3, 2)
FAR = (3, 2, 1)
TAIL = 8
TAIL16 = 16

VM = pl.BlockSpec(memory_space=pltpu.VMEM)
SM = pl.BlockSpec(memory_space=pltpu.SMEM)
ANY = pl.BlockSpec(memory_space=pl.ANY)
BLOCK = pl.BlockSpec((ROWS, WIDE), lambda i: (0, i))
STATE = jax.ShapeDtypeStruct((GROUP, DH, DH), BF16)


def params():
    return pltpu.CompilerParams(vmem_limit_bytes=LIMIT)


def cost(flops, nbytes, trans=0):
    return pl.CostEstimate(flops=flops, bytes_accessed=nbytes, transcendentals=trans)


def split(x):
    hi = x.astype(BF16)
    return hi, (x - hi.astype(F32)).astype(BF16)


def dot(a, b, dims):
    return lax.dot_general(a, b, (dims, ((), ())), preferred_element_type=F32)


def iota2(axis):
    return lax.broadcasted_iota(jnp.int32, (ROWS, ROWS), axis)


def exact(a, b):
    return lax.dot_general(
        a, b, (((1,), (0,)), ((), ())), precision=HIGHEST, preferred_element_type=F32
    )


def near_kernel(ld_ref, out_ref):
    for j in range(NZ):
        out_ref[j, :GROUP, :] = ld_ref[j]
        out_ref[j, GROUP:, :] = ld_ref[j ^ 1]


def with_near(ld):
    return pl.pallas_call(
        near_kernel,
        in_specs=[VM],
        out_specs=VM,
        out_shape=jax.ShapeDtypeStruct((NZ, 2 * GROUP, ROWS), F32),
        compiler_params=params(),
        cost_estimate=cost(0, 1 << 17),
    )(ld)


def state_kernel(count, chunks, k_ref, v_ref, ld_ref, *refs):
    outs, held, sems = refs[:count], refs[count], refs[count + 1]
    step = pl.program_id(0)
    later = (iota2(0) > iota2(1)).astype(F32)
    carried = jnp.exp(jnp.minimum(exact(ld_ref[0], later), 0.0))
    for i in range(GROUP):
        cols = slice(i * DH, (i + 1) * DH)
        hi, lo = split(k_ref[:, cols].astype(F32).T * carried[i : i + 1, :])
        v = v_ref[:, cols]
        both = jnp.concatenate([hi, lo], axis=1)
        held[step, i] = dot(both, jnp.concatenate([v, v], axis=0), ((1,), (0,))).astype(BF16)
    copies = [pltpu.make_async_copy(held.at[k], outs[k], sems.at[k]) for k in range(count)]
    for k in range(count):

        @pl.when(step == k)
        def _():
            copies[k].start()

    @pl.when(step == count - 1)
    def _():
        for copy in copies:
            copy.wait()


def block_states(chunks, count, k, v, ld):
    wide = pl.BlockSpec((ROWS, WIDE), lambda i, c: (0, c[i]))
    return pl.pallas_call(
        functools.partial(state_kernel, count),
        grid_spec=pltpu.PrefetchScalarGridSpec(
            num_scalar_prefetch=1,
            grid=(count,),
            in_specs=[wide, wide, pl.BlockSpec((1, GROUP, ROWS), lambda i, c: (c[i], 0, 0))],
            out_specs=[ANY] * count,
            scratch_shapes=[
                pltpu.VMEM((count, GROUP, DH, DH), BF16),
                pltpu.SemaphoreType.DMA((count,)),
            ],
        ),
        out_shape=[STATE] * count,
        compiler_params=params(),
        cost_estimate=cost(count * GROUP * 4 * 128**3, count * 800000, 1 << 10),
    )(chunks, k, v, ld)


def intra_kernel(q_ref, k_ref, v_ref, ld_ref, after_ref, out_ref, qd_ref):
    ld = ld_ref[0]
    cum_t = exact(ld, (iota2(0) <= iota2(1)).astype(F32))
    causal = iota2(0) >= iota2(1)
    for i in range(GROUP):
        cols = slice(i * DH, (i + 1) * DH)
        across = jnp.broadcast_to(cum_t[i : i + 1, :], (ROWS, ROWS))
        down = across.T
        weight = jnp.where(causal, jnp.exp(jnp.minimum(down - across, 0.0)), 0.0)
        q = q_ref[:, cols]
        scores = dot(q, k_ref[:, cols], ((1,), (1,)))
        hi, lo = split(scores * weight)
        v = v_ref[:, cols]
        both = jnp.concatenate([hi, lo], axis=1)
        out_ref[:, cols] = dot(both, jnp.concatenate([v, v], axis=0), ((1,), (0,)))
        hi, lo = split(q.astype(F32) * jnp.exp(down))
        qd_ref[:, 2 * i * DH : (2 * i + 1) * DH] = hi
        qd_ref[:, (2 * i + 1) * DH : (2 * i + 2) * DH] = lo


def intra(q, k, v, ld, after):
    return pl.pallas_call(
        intra_kernel,
        grid=(NZ,),
        in_specs=[BLOCK, BLOCK, BLOCK, pl.BlockSpec((1, GROUP, ROWS), lambda i: (i, 0, 0)), ANY],
        out_specs=[BLOCK, pl.BlockSpec((ROWS, 2 * WIDE), lambda i: (0, i))],
        out_shape=[
            jax.ShapeDtypeStruct((ROWS, NZ * WIDE), F32),
            jax.ShapeDtypeStruct((ROWS, 2 * NZ * WIDE), BF16),
        ],
        compiler_params=params(),
        cost_estimate=cost(64 * 6 * 128**3, 14 << 20, 1 << 21),
    )(q, k, v, ld, after)


def signed(place):
    return 1 - 2 * lax.rem(place[0], 2)


def group_at(place, a):
    return lax.rem(place[0] + 2 * NZ - signed(place) * a, NZ)


def pair_behind(place, a):
    own = place[0] // 2
    return lax.rem(own + 4 + {1: -1, 2: 1, 3: 2}[a] * signed(place), 4)


def join_kernel(a, place, d_ref, keep_ref, got_ref, *refs):
    out_ref = refs[-1]
    even = lax.rem(place[0], 2) == 0
    group = group_at(place, a)
    for h in range(GROUP):
        keep, got = keep_ref[h].astype(F32), got_ref[h].astype(F32)
        first, second = jnp.where(even, keep, got), jnp.where(even, got, keep)
        out_ref[h] = (first * d_ref[group * GROUP + h] + second).astype(BF16)


def join(a, place, over_odd, keep, got, after):
    return pl.pallas_call(
        functools.partial(join_kernel, a),
        in_specs=[SM, SM, VM, VM] + [ANY] * len(after),
        out_specs=VM,
        out_shape=STATE,
        compiler_params=params(),
        cost_estimate=cost(GROUP * DH * DH * 4, 800000),
    )(place, over_odd, keep, got, *after)


def part_kernel(a, place, d_ref, start_ref, keep_ref, got_ref, *refs):
    own_ref, pass_ref = refs[-2:]
    even = lax.rem(place[0], 2) == 0
    group = group_at(place, a)
    for h in range(GROUP):
        start = start_ref[h].astype(F32)
        state = jnp.where(even, keep_ref[h].astype(F32), got_ref[h].astype(F32))
        later = start * d_ref[group * GROUP + h] + state
        own_ref[h] = jnp.where(even, start, later).astype(BF16)
        pass_ref[h] = jnp.where(even, later, start).astype(BF16)


def part(a, place, over_even, start, keep, got, after):
    return pl.pallas_call(
        functools.partial(part_kernel, a),
        in_specs=[SM, SM, VM, VM, VM] + [ANY] * len(after),
        out_specs=[VM, VM],
        out_shape=[STATE, STATE],
        compiler_params=params(),
        cost_estimate=cost(GROUP * DH * DH * 4, 1300000),
    )(place, over_even, start, keep, got, *after)


def row_kernel(place, w_ref, r_ref, own_ref, near_ref, *refs):
    far, sides = refs[: len(FAR)], refs[-2:]
    z, core = place[0], place[1]
    pieces = [(own_ref, z), (near_ref, z + signed(place))]
    pieces += [(ref, 2 * pair_behind(place, a) + 1) for a, ref in zip(FAR, far)]
    for ref, side in zip(sides, (core, 1 - core)):
        for i in range(PAIR):
            h = side * PAIR + i
            total = None
            for piece, block in pieces:
                term = piece[h].astype(F32) * w_ref[block * GROUP + h]
                total = term if total is None else total + term
            ref[i, :DH, :] = total
            ref[i, DH:, :] = jnp.full((TAIL, DH), r_ref[h], F32)


def row_states(place, weights, rows, pieces):
    shape = jax.ShapeDtypeStruct((PAIR, DH + TAIL, DH), F32)
    return pl.pallas_call(
        row_kernel,
        in_specs=[SM, SM, SM] + [VM] * len(pieces),
        out_specs=[VM, VM],
        out_shape=[shape, shape],
        compiler_params=params(),
        cost_estimate=cost(GROUP * DH * DH * 10, 2 << 20),
    )(place, weights, rows, *pieces)


def put(ref, i, state, decay):
    hi = decay.astype(BF16).astype(F32)
    mid = (decay - hi).astype(BF16).astype(F32)
    low = decay - hi - mid
    row = lax.broadcasted_iota(jnp.int32, (TAIL16, DH), 0)
    tail = jnp.where(row == 0, hi, jnp.where(row == 1, mid, jnp.where(row == 2, low, 0.0)))
    ref[i, :DH, :] = state.astype(BF16)
    ref[i, DH:, :] = tail.astype(BF16)


def decay_of(ref, i):
    return jnp.sum(ref[i, DH:, :].astype(F32), axis=0, keepdims=True)


def picked(values, flags):
    total = jnp.zeros_like(values[0])
    for value, flag in zip(values, flags):
        total = total + jnp.where(flag, value, 0.0)
    return total


def behind(at, n):
    return [lax.rem(at + n - k, n) for k in STEPS]


def ordered(core, mine_ref, got_ref, i):
    first = jnp.where(core == 0, mine_ref[i], got_ref[i])
    second = jnp.where(core == 0, got_ref[i], mine_ref[i])
    return first[:DH], first[DH : DH + 1], second[:DH], second[DH : DH + 1]


def pair_kernel(place, mine_ref, got_ref, out_ref):
    for i in range(PAIR):
        first, over_first, second, over_second = ordered(place[1], mine_ref, got_ref, i)
        put(out_ref, i, jnp.exp(over_second) * first + second, over_first + over_second)


def line_kernel(place, *refs):
    pairs, out_ref = refs[:NY], refs[-1]
    ys = behind(place[3], NY)
    for i in range(PAIR):
        decays = [decay_of(p, i) for p in pairs]
        total = None
        for k in range(NY):
            gap = picked(decays, [other > ys[k] for other in ys])
            term = jnp.exp(gap) * pairs[k][i, :DH, :].astype(F32)
            total = term if total is None else total + term
        put(out_ref, i, total, sum(decays))


def entry_kernel(place, start_ref, mine_ref, got_ref, *refs):
    pairs, lines, (keep_ref, give_ref) = refs[:NY], refs[NY : NY + NX], refs[-2:]
    core, x, y = place[1], place[2], place[3]
    xs, ys = behind(x, NX), behind(y, NY)
    for i in range(PAIR):
        over_pairs = [decay_of(p, i) for p in pairs]
        over_lines = [decay_of(p, i) for p in lines]
        in_line = picked(over_pairs, [at < y for at in ys])
        gap = in_line + picked(over_lines, [at < x for at in xs])
        entry = jnp.exp(gap) * start_ref[core * PAIR + i]
        for k in range(1, NY):
            gap = picked(over_pairs, [(at > ys[k]) & (at < y) for at in ys])
            weight = jnp.where(ys[k] < y, jnp.exp(gap), 0.0)
            entry = entry + weight * pairs[k][i, :DH, :].astype(F32)
        for k in range(1, NX):
            gap = in_line + picked(over_lines, [(at > xs[k]) & (at < x) for at in xs])
            weight = jnp.where(xs[k] < x, jnp.exp(gap), 0.0)
            entry = entry + weight * lines[k][i, :DH, :].astype(F32)
        first, over_first, _, _ = ordered(core, mine_ref, got_ref, i)
        later = jnp.exp(over_first) * entry + first
        keep_ref[i] = jnp.where(core == 0, entry, later)
        give_ref[i] = jnp.where(core == 0, later, entry)


def small(kernel, out_shape, place, *args):
    single = not isinstance(out_shape, list)
    return pl.pallas_call(
        kernel,
        in_specs=[SM] + [VM] * len(args),
        out_specs=VM if single else [VM] * len(out_shape),
        out_shape=out_shape,
        compiler_params=params(),
        cost_estimate=cost(PAIR * DH * DH * 16, 1 << 20),
    )(place, *args)


def seq_scan(place, mine, give, start):
    message = jax.ShapeDtypeStruct((PAIR, DH + TAIL16, DH), BF16)
    state = jax.ShapeDtypeStruct((PAIR, DH, DH), F32)
    got = swap_core(give)
    pairs = around(small(pair_kernel, message, place, mine, got), from_y, NY)
    lines = around(small(line_kernel, message, place, *pairs), from_x, NX)
    keep, give = small(
        entry_kernel, [state, state], place, start, mine, got, *pairs, *lines
    )
    return keep, swap_core(give)


def spread_kernel(place, d_ref, keep_ref, got_ref, own_ref, near_ref, *refs):
    far, (out_own, out_near, *out_far) = refs[: len(FAR)], refs[len(FAR) : -2]
    states, entries = refs[-2], refs[-1]
    z, core = place[0], place[1]
    even, own = lax.rem(z, 2) == 0, z // 2
    for a, ref in zip(FAR, far):
        states[pair_behind(place, a)] = ref[...].astype(F32)
    for h in range(GROUP):
        mine, near = own_ref[h].astype(F32), near_ref[h].astype(F32)
        first, second = jnp.where(even, mine, near), jnp.where(even, near, mine)
        states[own, h] = first * d_ref[(2 * own + 1) * GROUP + h] + second
    for ref, side in ((keep_ref, core), (got_ref, 1 - core)):
        for i in range(PAIR):
            h = side * PAIR + i
            state = ref[i]
            for p in range(NZ // 2):
                entries[p, h] = state
                if p < NZ // 2 - 1:
                    over = d_ref[2 * p * GROUP + h] * d_ref[(2 * p + 1) * GROUP + h]
                    state = state * over + states[p, h]
    for a, out in zip(FAR, out_far):
        out[...] = entries[pair_behind(place, a)].astype(BF16)
    for h in range(GROUP):
        start = entries[own, h]
        first = jnp.where(even, own_ref[h].astype(F32), near_ref[h].astype(F32))
        later = start * d_ref[2 * own * GROUP + h] + first
        out_own[h] = jnp.where(even, start, later).astype(BF16)
        out_near[h] = jnp.where(even, later, start).astype(BF16)


def spread(place, decays, keep, got, pieces):
    count = len(pieces)
    return pl.pallas_call(
        spread_kernel,
        in_specs=[SM, SM] + [VM] * (2 + count),
        out_specs=[VM] * count,
        out_shape=[STATE] * count,
        scratch_shapes=[pltpu.VMEM((NZ // 2, GROUP, DH, DH), F32)] * 2,
        compiler_params=params(),
        cost_estimate=cost(GROUP * DH * DH * 16, 5 << 20),
    )(place, decays, keep, got, *pieces)


def finish_kernel(count, chunks, *refs):
    qd_ref, o_ref, *entries = refs[-4 - count : -2]
    out_ref, held = refs[-2], refs[-1]
    step = pl.program_id(0)
    for k in range(count):

        @pl.when(step == k)
        def _():
            for i in range(GROUP):
                cols = slice(i * DH, (i + 1) * DH)
                entry = entries[k][i]
                far = dot(
                    qd_ref[:, 2 * i * DH : (2 * i + 2) * DH],
                    jnp.concatenate([entry, entry], axis=0),
                    ((1,), (0,)),
                )
                held[i * ROWS : (i + 1) * ROWS, :] = o_ref[:, cols] + far

    o = held[...]
    ones = jnp.ones((2 * DH, DH), BF16)
    mean = dot(jnp.concatenate(split(o * o), axis=1), ones, ((1,), (0,))) * (1.0 / DH)
    o = (o * lax.rsqrt(mean + 1e-5)).astype(BF16)
    for i in range(GROUP):
        out_ref[:, i * DH : (i + 1) * DH] = o[i * ROWS : (i + 1) * ROWS, :]


def finish(chunks, qd, o, entries, held):
    count = len(entries)
    wide = pl.BlockSpec((ROWS, WIDE), lambda i, c: (0, c[i]))
    specs = [] if held is None else [ANY]
    specs += [pl.BlockSpec((ROWS, 2 * WIDE), lambda i, c: (0, c[i])), wide]
    specs += [pl.BlockSpec((GROUP, DH, DH), lambda i, c: (0, 0, 0))] * count
    args = [chunks] + ([] if held is None else [held]) + [qd, o, *entries]
    aliases = {} if held is None else {1: 0}
    return pl.pallas_call(
        functools.partial(finish_kernel, count),
        grid_spec=pltpu.PrefetchScalarGridSpec(
            num_scalar_prefetch=1,
            grid=(count,),
            in_specs=specs,
            out_specs=wide,
            scratch_shapes=[pltpu.VMEM((GROUP * ROWS, DH), F32)],
        ),
        out_shape=jax.ShapeDtypeStruct(o.shape, BF16),
        input_output_aliases=aliases,
        compiler_params=params(),
        cost_estimate=cost(8 * count * 4 * 128**3, count * 1500000, 1 << 14),
    )(*args)


def swap_near(a):
    return lax.ppermute(a, "head", [(i, i ^ 1) for i in range(NZ)])


def hops(a):
    return [(i, (i + (a if i % 2 else -a)) % NZ) for i in range(NZ)]


def to_owner(x, a):
    return lax.ppermute(x, "head", hops(a))


def from_owner(x, a):
    return lax.ppermute(x, "head", [(j, i) for i, j in hops(a)])


def seq_index(x, y, core):
    return (x * NY + y) * 2 + core


def swap_core(a):
    return lax.ppermute(a, "seq", [(i, i ^ 1) for i in range(NX * NY * 2)])


def from_y(a, k):
    pairs = [
        (seq_index(x, y, c), seq_index(x, (y + k) % NY, c))
        for x in range(NX)
        for y in range(NY)
        for c in range(2)
    ]
    return lax.ppermute(a, "seq", pairs)


def from_x(a, k):
    pairs = [
        (seq_index(x, y, c), seq_index((x + k) % NX, y, c))
        for x in range(NX)
        for y in range(NY)
        for c in range(2)
    ]
    return lax.ppermute(a, "seq", pairs)


def around(a, move, n):
    return [a] + [move(a, k) for k in STEPS[1:]]


def local(queries, key_rows, value_rows, log_decay, initial_state):
    queries, key_rows, value_rows = (
        pltpu.with_memory_space_constraint(a, pltpu.HBM) for a in (queries, key_rows, value_rows)
    )
    z = lax.axis_index("head").astype(jnp.int32)
    s = lax.axis_index("seq").astype(jnp.int32)
    place = jnp.stack([z, s % 2, s // (2 * NY), (s // 2) % NY])
    by_block = jnp.swapaxes(log_decay.T.reshape(GROUP, NZ, ROWS), 0, 1)
    ld = lax.all_to_all(with_near(by_block), "head", 0, 0, tiled=True)

    total = jnp.sum(by_block, axis=2)
    cells = jnp.arange(NZ)
    after = (cells[None, :] > cells[:, None])[..., None]
    closing = jnp.exp(jnp.sum(jnp.where(after, total[None], 0.0), axis=1)).reshape(-1)
    decays = jnp.exp(total).reshape(-1)
    rows = jnp.sum(total, axis=0)

    sign = 1 - 2 * (z % 2)

    def keeps(*turns):
        return [(z - sign * a) % NZ for a in turns]

    def gives(*turns):
        return [(z + sign * a) % NZ for a in turns]

    over = jnp.sum(ld, axis=2)
    mine_over, near_over = over[:, :GROUP].reshape(-1), over[:, GROUP:].reshape(-1)
    over_even = jnp.exp(jnp.where(z % 2 == 0, mine_over, near_over))
    over_odd = jnp.exp(jnp.where(z % 2 == 0, near_over, mine_over))

    give, kept, got, joined = {}, {}, {}, {}
    give[4], give[3] = block_states(jnp.stack(gives(4, 3)), 2, key_rows, value_rows, ld)
    kept[3], give[2], give[1] = block_states(
        jnp.stack(keeps(3) + gives(2, 1)), 3, key_rows, value_rows, ld
    )
    kept[2], kept[1], kept[0] = block_states(
        jnp.stack(keeps(2, 1, 0)), 3, key_rows, value_rows, ld
    )
    for a in (3, 2, 1, 0):
        got[a] = swap_near(give[a + 1])
    after = []
    for a in FAR:
        pair = join(a, place, over_odd, kept[a], got[a], after)
        joined[a], after = to_owner(pair, a), [pair]

    pieces = [kept[0], got[0]] + [joined[a] for a in FAR]
    mine, other = row_states(place, closing, rows, pieces)
    keep, other = seq_scan(place, mine, other, initial_state)
    entry = {}
    own, near, *far = spread(place, decays, keep, other, pieces)
    o, qd = intra(queries, key_rows, value_rows, ld, own)
    entry[0] = own
    near = swap_near(near)
    sent = {a: from_owner(x, a) for a, x in zip(FAR, far)}
    passed = {}

    def pass_on(a, after):
        entry[a], x = part(a, place, over_even, sent[a], kept[a], got[a], after)
        passed[a] = swap_near(x)

    pass_on(2, [qd])
    pass_on(1, [qd])
    early = [entry[0], near, entry[1], entry[2]]
    out = finish(jnp.stack(keeps(0) + gives(1) + keeps(1, 2)), qd, o, early, None)
    pass_on(3, [out])
    middle = [entry[3], passed[2], passed[1]]
    out = finish(jnp.stack(keeps(3) + gives(3, 2)), qd, o, middle, out)
    return finish(jnp.stack(gives(4)), qd, o, [passed[3]], out)


def solution(mesh):
    placed = (
        P(("seq", "head"), None),
        P(("seq", "head"), None),
        P(("seq", "head"), None),
        P("seq", "head"),
        P("head", None, None),
    )
    return jax.shard_map(
        local, mesh=mesh, in_specs=placed, out_specs=P(("seq", "head"), None), check_vma=False
    )
```
